512 devices in a mesh: freq: 64 (over x, z_lo, core), tm: 4 (over y), tile: 2 (over z_hi).
Axes of the slice: x: 4, y: 4, z: 16 (z_hi: 2, z_lo: 8; z = z_hi * 8 + z_lo), core: 2. Of those that a mesh axis runs over, the one named last changes fastest.
Arguments:
- samples: bfloat16 [2048, 32, 2048], P('freq', ('tm', 'tile'))
- prototype: float32 [4, 2048], replicated, may hold values from -3 to 3
- feed_map: int32 [2048], replicated, may hold values from 0 to 2047, each once
- keep_mask: int32 [2048], replicated, may hold values 0 or 1
- tile_pairs: int32 [16, 2], replicated, may hold values from 0 to 31, as said below
Outputs:
- visibilities: float32 [16, 1024, 64, 128], P(('tm', 'tile'), 'freq')
The draws below stay inside these ranges and needn't reach their ends.
Inputs may be any that keep to these rules, and one draw needn't show every extreme that they name: `tile_pairs`: each row is a pair of tile numbers below 32 with the first not above the second; no two rows are equal; every tile number appears in some row.
All inputs are finite; a program needn't handle non-finite values.
Results may differ from the reference program's by a relative error of at most 0.012.
Values may be sent and summed in bfloat16 or wider, within the bound.
A program may use at most 64 MiB of HBM per device.

```python
import math
import jax
import jax.numpy as jnp
import numpy as np
from jax import lax

NI = 2048
NP = 2048
NCH = 1024
TAPS = 4
B = 64
FRD = 4
TILES = 16
FRAMES = 32
N_FREQ = 64


def draw_samples(key, part):
    key = jax.random.fold_in(key, 1)
    sky_key, noise_key = jax.random.split(key, 2)
    sky = jax.random.normal(sky_key, (1, FRAMES, NP), jnp.float32)
    noise = jax.random.normal(noise_key, (NI, FRAMES, NP), jnp.float32)
    return (0.6 * sky + 0.8 * noise).astype(jnp.bfloat16)


def draw_tile_pairs(key, part):
    key = jax.random.fold_in(key, 2)
    match_key, rest_key, order_key = jax.random.split(key, 3)
    sides = NI // B
    firsts = np.array([r for r in range(sides) for c in range(r, sides)], dtype=np.int32)
    seconds = np.array([c for r in range(sides) for c in range(r, sides)], dtype=np.int32)
    count = firsts.shape[0]
    shuffled = jax.random.permutation(match_key, sides).astype(jnp.int32).reshape(sides // 2, 2)
    lower = jnp.minimum(shuffled[:, 0], shuffled[:, 1])
    upper = jnp.maximum(shuffled[:, 0], shuffled[:, 1])
    matched = (lower * sides - lower * (lower - 1) // 2 + (upper - lower)).astype(jnp.int32)
    candidates = jax.random.permutation(rest_key, count).astype(jnp.int32)
    taken = jnp.any(candidates[:, None] == matched[None, :], axis=1).astype(jnp.int32)
    order = jnp.argsort(taken, stable=True)
    others = candidates[order][:TILES - sides // 2]
    chosen = jnp.concatenate([matched, others]).astype(jnp.int32)
    chosen = chosen[jax.random.permutation(order_key, TILES)]
    return jnp.stack([jnp.asarray(firsts)[chosen], jnp.asarray(seconds)[chosen]], axis=1).astype(jnp.int32)


def place_ends(values, stream_key, smallest, largest):
    index_at = [jax.random.randint(jax.random.fold_in(stream_key, axis), (), 0, length) for axis, length in enumerate(values.shape)]
    longest = values.shape.index(max(values.shape))
    neighbour = index_at[:longest] + [(index_at[longest] + 1) % values.shape[longest]] + index_at[longest + 1:]
    return values.at[tuple(index_at)].set(smallest).at[tuple(neighbour)].set(largest)


def gaussian(rng, dims, spread, limit, kind=jnp.bfloat16):
    values = jax.random.normal(rng, dims, jnp.float32) * spread
    return jnp.minimum(jnp.maximum(values, -limit), limit).astype(kind)


def setup_inputs(seed: int = 0) -> dict:
    seeds = jax.random.split(jax.random.key(seed), 6)
    samples = draw_samples(jax.random.fold_in(seeds[5], 71), 0)
    prototype = gaussian(seeds[1], (TAPS, NP), 0.5, 3.0, jnp.float32)
    feed_map = jax.random.permutation(seeds[2], NI).astype(jnp.int32)
    keep_mask = place_ends((jax.random.randint(seeds[3], (NI,), 0, 8) < 7).astype(jnp.int32), jax.random.fold_in(seeds[3], 1), 0, 1)
    tile_pairs = draw_tile_pairs(jax.random.fold_in(seeds[5], 71), 0)
    return {"samples": samples, "prototype": prototype, "feed_map": feed_map, "keep_mask": keep_mask, "tile_pairs": tile_pairs}


def dft_table(points):
    rows = lax.broadcasted_iota(jnp.int32, (points, points), 0)
    columns = lax.broadcasted_iota(jnp.int32, (points, points), 1)
    phase = rows * (columns // 2) % points
    angle = phase.astype(jnp.float32) * (2.0 * math.pi / points)
    scale = 1.0 / math.sqrt(points)
    value = jnp.where(columns % 2 == 0, jnp.cos(angle), -jnp.sin(angle)) * scale
    return value.astype(jnp.bfloat16)

def filter_block(block, prototype):
    taps = prototype.shape[0]
    frames = block.shape[1]
    padded = jnp.pad(block, ((0, 0), (taps - 1, 0), (0, 0)))
    total = jnp.zeros(block.shape, jnp.float32)
    for lag in range(taps):
        total = total + prototype[lag] * padded[:, taps - 1 - lag:taps - 1 - lag + frames].astype(jnp.float32)
    return total.astype(jnp.bfloat16)

def reference(samples, prototype, feed_map, keep_mask, tile_pairs):
    table = dft_table(NP)
    blocks = samples.reshape(N_FREQ, NI // N_FREQ, FRAMES, NP)

    def channelize(block):
        filtered = filter_block(block, prototype)
        spectra = jnp.dot(filtered.reshape(-1, NP), table, preferred_element_type=jnp.float32)
        return spectra.astype(jnp.bfloat16).reshape(block.shape[0], FRAMES, NCH, 2)
    channels = lax.map(channelize, blocks).reshape(NI, FRAMES, NCH, 2)
    offsets = jnp.arange(B, dtype=jnp.int32)

    def one_tile(pair):
        row_feeds = feed_map[pair[0] * B + offsets]
        col_feeds = feed_map[pair[1] * B + offsets]
        left_side = channels[row_feeds].astype(jnp.float32).reshape(B, FRAMES // FRD, FRD, NCH, 2)
        right_side = channels[col_feeds].astype(jnp.float32).reshape(B, FRAMES // FRD, FRD, NCH, 2)
        swapped = jnp.stack([left_side[..., 1], -left_side[..., 0]], axis=-1)
        real_part = jnp.einsum('akfcp,bkfcp->kcab', left_side, right_side)
        imaginary = jnp.einsum('akfcp,bkfcp->kcab', swapped, right_side)
        weight = keep_mask[row_feeds].astype(jnp.float32)[:, None] * keep_mask[col_feeds].astype(jnp.float32)[None, :]
        weight = jnp.concatenate([weight, weight], axis=1)
        partial_value = (jnp.concatenate([real_part, imaginary], axis=-1) * weight).astype(jnp.bfloat16)
        partial_value = lax.optimization_barrier(partial_value)
        return lax.optimization_barrier(jnp.sum(partial_value.astype(jnp.float32), axis=0)) / FRAMES
    return lax.map(one_tile, tile_pairs)
```

```python
import math

import jax
import jax.numpy as jnp
import numpy as np
from jax import lax
from jax.sharding import PartitionSpec as P

B = 64


def from_behind(value, axis, by):
    length = lax.axis_size(axis)
    pairs = [(i, i + by) for i in range(length) if 0 <= i + by < length]
    return lax.ppermute(value, axis, pairs)


def dft_table(points):
    rows = np.arange(points)[:, None]
    columns = np.arange(points)[None, :]
    angle = (rows * (columns // 2) % points) * (2.0 * math.pi / points)
    value = np.where(columns % 2 == 0, np.cos(angle), -np.sin(angle)) / math.sqrt(points)
    return jnp.asarray(value.astype(np.float32)).astype(jnp.bfloat16)


def shards(samples, prototype, feed_map, keep_mask, tile_pairs):
    taps = prototype.shape[0]
    inputs_local, frames_local, points = samples.shape
    groups = lax.axis_size("freq")
    nodes = lax.axis_size(("tm", "tile"))
    per_group = points // 2 // groups
    total_inputs = inputs_local * groups
    leading = from_behind(samples[:, frames_local - (taps - 1) :, :], ("tm", "tile"), 1)
    extended = jnp.concatenate([leading, samples], axis=1)
    total = jnp.zeros(samples.shape, jnp.float32)
    for lag in range(taps):
        total = total + prototype[lag] * extended[
            :, taps - 1 - lag : taps - 1 - lag + frames_local
        ].astype(jnp.float32)
    filtered = total.astype(jnp.bfloat16)
    spectra = jnp.dot(
        filtered.reshape(-1, points), dft_table(points), preferred_element_type=jnp.float32
    )
    spectra = spectra.astype(jnp.bfloat16)
    outgoing = spectra.reshape(inputs_local, frames_local, groups, 2 * per_group).transpose(
        2, 0, 1, 3
    )
    outgoing = outgoing.reshape(groups * inputs_local, frames_local * 2 * per_group)
    voltages = lax.all_to_all(outgoing, "freq", split_axis=0, concat_axis=0, tiled=True)

    sides = tile_pairs.reshape(-1)
    hit = sides[:, None] == jnp.arange(total_inputs // B, dtype=jnp.int32)[None, :]
    feeds = jnp.sum(
        jnp.where(hit[:, :, None], feed_map.reshape(1, -1, B), 0), axis=1
    ).reshape(-1)
    place = jnp.where(
        feeds[:, None] == jnp.arange(total_inputs, dtype=jnp.int32)[None, :],
        keep_mask[None, :],
        0,
    ).astype(jnp.bfloat16)
    ordered = jnp.dot(place, voltages, preferred_element_type=jnp.float32).astype(jnp.bfloat16)
    field = lax.all_to_all(ordered, ("tm", "tile"), split_axis=0, concat_axis=0, tiled=True)
    tiles = tile_pairs.shape[0] // nodes
    field = field.reshape(nodes, tiles, 2, B, frames_local, per_group, 2)
    left, right = field[:, :, 0], field[:, :, 1]
    turned = jnp.stack([-right[..., 1], right[..., 0]], axis=-1)
    doubled = jnp.concatenate([right, turned], axis=2)
    product = jnp.einsum(
        "ntafcp,ntbfcp->tcab", left, doubled, preferred_element_type=jnp.float32
    )
    return product / (frames_local * nodes)


def solution(mesh):
    placed = (P("freq", ("tm", "tile"), None), P(), P(), P(), P())
    return jax.shard_map(
        shards,
        mesh=mesh,
        in_specs=placed,
        out_specs=P(("tm", "tile"), "freq", None, None),
        check_vma=False,
    )
```

```python
import math

import jax
import jax.numpy as jnp
import numpy as np
from jax import lax
from jax.experimental import pallas as pl
from jax.experimental.pallas import tpu as pltpu
from jax.sharding import PartitionSpec as P

MESH = pl.DeviceIdType.MESH
B = 64
HALF = 16
LANES = 128


def dft_table(points, groups):
    per_group = points // 2 // groups
    column = np.arange(points)
    group, rest = column // (2 * per_group), column % (2 * per_group)
    part, channel = rest // per_group, group * per_group + rest % per_group
    angle = (np.arange(points)[:, None] * channel[None, :] % points) * (2.0 * math.pi / points)
    value = np.where(part[None, :] == 0, np.cos(angle), -np.sin(angle)) / math.sqrt(points)
    return jnp.asarray(value.astype(np.float32)).astype(jnp.bfloat16)


def kernel(
    sizes,
    x_ref,
    proto_ref,
    table_hbm,
    feeds_ref,
    source_ref,
    keep_lane_ref,
    out_ref,
    table_ref,
    place_ref,
    halo_ref,
    filt_ref,
    turn_out,
    turn_in,
    cat_ref,
    tile_out,
    tile_in,
    left_ref,
    right_ref,
    table_sem,
    halo_send,
    halo_recv,
    turn_send,
    turn_recv,
    tile_send,
    tile_recv,
):
    groups, n_tm, n_tile = sizes
    nodes = n_tm * n_tile
    me, tm, tile = lax.axis_index("freq"), lax.axis_index("tm"), lax.axis_index("tile")
    node = tm * n_tile + tile
    frames, inputs, points = x_ref.shape

    def node_id(k):
        return (me, lax.div(k, n_tile), lax.rem(k, n_tile))

    table_copy = pltpu.make_async_copy(table_hbm, table_ref, table_sem)
    table_copy.start()

    barrier = pltpu.get_barrier_semaphore()

    def greet_group(k, carry):
        pl.semaphore_signal(
            barrier, 1, device_id=(lax.rem(me + k, groups), tm, tile), device_id_type=MESH
        )
        return carry

    def greet_node(k, carry):
        pl.semaphore_signal(
            barrier, 1, device_id=node_id(lax.rem(node + k, nodes)), device_id_type=MESH
        )
        return carry

    lax.fori_loop(1, nodes, greet_node, 0)
    lax.fori_loop(1, groups, greet_group, 0)
    pl.semaphore_wait(barrier, groups - 1 + nodes - 1)

    def halo_copy(j):
        return pltpu.make_async_remote_copy(
            src_ref=x_ref.at[j + 1],
            dst_ref=halo_ref.at[j],
            send_sem=halo_send.at[j],
            recv_sem=halo_recv.at[j],
            device_id=node_id(lax.rem(node + 1, nodes)),
            device_id_type=MESH,
        )

    taps = proto_ref.shape[0]

    @pl.when(node < nodes - 1)
    def _():
        for j in range(taps - 2, -1, -1):
            halo_copy(j).start()

    def build(k, carry):
        rows = pl.ds(pl.multiple_of(k * 128, 128), 128)
        hit = feeds_ref[rows, :] == source_ref[...]
        place_ref[rows, :] = jnp.where(hit, 1.0, 0.0).astype(jnp.bfloat16)
        return carry

    lax.fori_loop(0, place_ref.shape[0] // 128, build, 0)

    def wait_halo(j):
        @pl.when(node == 0)
        def _():
            halo_ref[j] = jnp.zeros(halo_ref.shape[1:], halo_ref.dtype)

        @pl.when(node > 0)
        def _():
            halo_copy(j).wait_recv()

    def filter_frame(j, row):
        def columns(q, carry):
            cols = pl.ds(pl.multiple_of(q * 512, 512), 512)
            total = None
            for lag in range(taps):
                k = j - lag
                frame = x_ref[k, :, cols] if k >= 0 else halo_ref[taps - 1 + k, :, cols]
                term = proto_ref[lag : lag + 1, cols] * frame.astype(jnp.float32)
                total = term if total is None else total + term
            filt_ref[row * inputs : (row + 1) * inputs, cols] = total.astype(jnp.bfloat16)
            return carry

        lax.fori_loop(0, points // 512, columns, 0)

    width = points // groups

    def channelize(chunk):
        def columns(q, carry):
            cols = pl.ds(pl.multiple_of(q * 256, 256), 256)
            y = jnp.dot(filt_ref[...], table_ref[:, cols], preferred_element_type=jnp.float32)
            for b in range(256 // width):
                pieces = [
                    y[f * inputs + i * HALF : f * inputs + (i + 1) * HALF, b * width : (b + 1) * width]
                    for i in range(2)
                    for f in range(2)
                ]
                turn_out[chunk, q * (256 // width) + b] = jnp.concatenate(pieces, axis=1).astype(
                    jnp.bfloat16
                )
            return carry

        lax.fori_loop(0, points // 256, columns, 0)

    def turn_copy(chunk, k):
        peer = lax.rem(me + k, groups)
        return pltpu.make_async_remote_copy(
            src_ref=turn_out.at[chunk, peer],
            dst_ref=turn_in.at[chunk, me],
            send_sem=turn_send.at[chunk],
            recv_sem=turn_recv.at[chunk],
            device_id=(peer, tm, tile),
            device_id_type=MESH,
        )

    def turn_all(chunk):
        return pltpu.make_async_remote_copy(
            src_ref=turn_out.at[chunk, pl.ds(0, groups - 1)],
            dst_ref=turn_in.at[chunk, pl.ds(0, groups - 1)],
            send_sem=turn_send.at[chunk],
            recv_sem=turn_recv.at[chunk],
            device_id=(lax.rem(me + 1, groups), tm, tile),
            device_id_type=MESH,
        )

    def send_turn(chunk):
        def go(k, carry):
            turn_copy(chunk, k).start()
            return carry

        lax.fori_loop(1, groups, go, 0)
        turn_in[chunk, me] = turn_out[chunk, me]

    def tile_copy(chunk, k):
        peer = lax.rem(node + k, nodes)
        return pltpu.make_async_remote_copy(
            src_ref=tile_out.at[chunk, peer],
            dst_ref=tile_in.at[chunk, node],
            send_sem=tile_send.at[chunk],
            recv_sem=tile_recv.at[chunk],
            device_id=node_id(peer),
            device_id_type=MESH,
        )

    def tile_all(chunk):
        return pltpu.make_async_remote_copy(
            src_ref=tile_out.at[chunk, pl.ds(0, nodes - 1)],
            dst_ref=tile_in.at[chunk, pl.ds(0, nodes - 1)],
            send_sem=tile_send.at[chunk],
            recv_sem=tile_recv.at[chunk],
            device_id=node_id(lax.rem(node + 1, nodes)),
            device_id_type=MESH,
        )

    rows_all = groups * HALF
    rows_node = tile_out.shape[2]
    per_step = 4

    def arrange(chunk):
        turn_all(chunk).wait_recv()
        block = turn_in[chunk].reshape(rows_all, LANES)
        turned = jnp.concatenate([block[:, B:], block[:, :B]], axis=1)
        cat_ref[0:rows_all] = block
        cat_ref[rows_all : 2 * rows_all] = turned
        low = lax.broadcasted_iota(jnp.int32, (per_step * rows_node, LANES), 1) < B

        def step(k, carry):
            size = per_step * rows_node
            first = pl.multiple_of(k * size, size)
            second = pl.multiple_of(nodes * rows_node + k * size, size)
            left = jnp.dot(
                place_ref[pl.ds(first, size), :], cat_ref[...], preferred_element_type=jnp.float32
            )
            right = jnp.dot(
                place_ref[pl.ds(second, size), :], cat_ref[...], preferred_element_type=jnp.float32
            )
            right = jnp.concatenate([right[:, B:], right[:, :B]], axis=1)
            both = jnp.where(low, left, right).astype(jnp.bfloat16)
            tile_out[chunk, pl.ds(k * per_step, per_step)] = both.reshape(
                per_step, rows_node, LANES
            )
            return carry

        lax.fori_loop(0, nodes // per_step, step, 0)

        def go(k, carry):
            tile_copy(chunk, k).start()
            return carry

        lax.fori_loop(1, nodes, go, 0)
        tile_in[chunk, node] = tile_out[chunk, node]

    filter_frame(3, 0)
    table_copy.wait()
    wait_halo(2)
    filter_frame(2, 1)
    channelize(0)
    send_turn(0)
    wait_halo(1)
    filter_frame(1, 0)
    wait_halo(0)
    filter_frame(0, 1)
    channelize(1)
    send_turn(1)
    arrange(0)
    arrange(1)

    tile_all(0).wait_recv()
    tile_all(1).wait_recv()
    lane = lax.broadcasted_iota(jnp.int32, (B, LANES), 1)
    low = lane < B
    channels = out_ref.shape[1]
    first_part = lax.rem(lane, 2 * channels) < channels
    for t in range(out_ref.shape[0]):
        for k in range(nodes):
            one = tile_in[0, k, t * B : (t + 1) * B, :].astype(jnp.float32)
            two = tile_in[1, k, t * B : (t + 1) * B, :].astype(jnp.float32)
            one_turned = pltpu.roll(one, B, 1)
            two_turned = pltpu.roll(two, B, 1)
            left = jnp.where(low, one, two_turned)
            right = jnp.where(low, one_turned, two)
            cross = jnp.where(
                first_part, -pltpu.roll(right, LANES - channels, 1), pltpu.roll(right, channels, 1)
            )
            cols = slice(k * LANES, (k + 1) * LANES)
            left_ref[:, cols] = left.astype(jnp.bfloat16)
            right_ref[0:B, cols] = right.astype(jnp.bfloat16)
            right_ref[B : 2 * B, cols] = cross.astype(jnp.bfloat16)
        masked = (left_ref[...][None] * keep_lane_ref[...][:, None, :]).reshape(
            channels * B, nodes * LANES
        )
        product = lax.dot_general(
            masked, right_ref[...], (((1,), (1,)), ((), ())), preferred_element_type=jnp.float32
        )
        out_ref[t] = (product * (1.0 / (frames * nodes))).reshape(channels, B, LANES)

    @pl.when(node < nodes - 1)
    def _():
        for j in range(taps - 2, -1, -1):
            halo_copy(j).wait_send()

    for chunk in range(2):
        turn_all(chunk).wait_send()
        tile_all(chunk).wait_send()


def solution(mesh):
    groups, n_tm, n_tile = mesh.shape["freq"], mesh.shape["tm"], mesh.shape["tile"]
    nodes = n_tm * n_tile

    def shards(samples, prototype, feed_map, keep_mask, tile_pairs):
        taps = prototype.shape[0]
        inputs, frames, points = samples.shape
        total = inputs * groups
        tiles = tile_pairs.shape[0] // nodes
        channels = points // 2 // groups
        sides = tile_pairs.T.reshape(-1)
        hit = sides[:, None] == jnp.arange(total // B, dtype=jnp.int32)[None, :]
        feeds = jnp.sum(
            jnp.where(hit[:, :, None], feed_map.reshape(1, -1, B), 0), axis=1
        ).reshape(-1, 1)
        source = jnp.where(keep_mask != 0, jnp.arange(total, dtype=jnp.int32), -1)
        source = source.reshape(groups, 2, HALF).transpose(1, 0, 2).reshape(1, total)
        lane = np.arange(nodes * LANES) % (B // 2)
        keep_lane = jnp.asarray(
            (lane[None, :] % channels == np.arange(channels)[:, None]).astype(np.float32)
        ).astype(jnp.bfloat16)
        vmem = pl.BlockSpec(memory_space=pltpu.VMEM)
        bf = jnp.bfloat16
        body = lambda *refs: kernel((groups, n_tm, n_tile), *refs)
        return pl.pallas_call(
            body,
            out_shape=jax.ShapeDtypeStruct((tiles, channels, B, 2 * B), jnp.float32),
            in_specs=[vmem, vmem, pl.BlockSpec(memory_space=pl.ANY), vmem, vmem, vmem],
            out_specs=vmem,
            scratch_shapes=[
                pltpu.VMEM((points, points), bf),
                pltpu.VMEM((total, total), bf),
                pltpu.VMEM((taps - 1, inputs, points), bf),
                pltpu.VMEM((2 * inputs, points), bf),
                pltpu.VMEM((2, groups, HALF, LANES), bf),
                pltpu.VMEM((2, groups, HALF, LANES), bf),
                pltpu.VMEM((2 * groups * HALF, LANES), bf),
                pltpu.VMEM((2, nodes, tiles * B, LANES), bf),
                pltpu.VMEM((2, nodes, tiles * B, LANES), bf),
                pltpu.VMEM((B, nodes * LANES), bf),
                pltpu.VMEM((2 * B, nodes * LANES), bf),
                pltpu.SemaphoreType.DMA,
                pltpu.SemaphoreType.DMA((taps - 1,)),
                pltpu.SemaphoreType.DMA((taps - 1,)),
                pltpu.SemaphoreType.DMA((2,)),
                pltpu.SemaphoreType.DMA((2,)),
                pltpu.SemaphoreType.DMA((2,)),
                pltpu.SemaphoreType.DMA((2,)),
            ],
            compiler_params=pltpu.CompilerParams(
                collective_id=0, has_side_effects=True, vmem_limit_bytes=48 * 2**20
            ),
            cost_estimate=pl.CostEstimate(flops=4 * 10**9, bytes_accessed=10**7, transcendentals=0),
        )(samples.transpose(1, 0, 2), prototype, dft_table(points, groups), feeds, source, keep_lane)

    return jax.shard_map(
        shards,
        mesh=mesh,
        in_specs=(P("freq", ("tm", "tile"), None), P(), P(), P(), P()),
        out_specs=P(("tm", "tile"), "freq", None, None),
        check_vma=False,
    )
```

```python
import math

import jax
import jax.numpy as jnp
import numpy as np
from jax import lax
from jax.experimental import pallas as pl
from jax.experimental.pallas import tpu as pltpu
from jax.sharding import PartitionSpec as P

MESH = pl.DeviceIdType.MESH
B = 64
HALF = 16
LANES = 128


def dft_table(points, groups):
    per_group = points // 2 // groups
    column = np.arange(points)
    group, rest = column // (2 * per_group), column % (2 * per_group)
    part, channel = rest // per_group, group * per_group + rest % per_group
    angle = (np.arange(points)[:, None] * channel[None, :] % points) * (2.0 * math.pi / points)
    value = np.where(part[None, :] == 0, np.cos(angle), -np.sin(angle)) / math.sqrt(points)
    return jnp.asarray(value.astype(np.float32)).astype(jnp.bfloat16)


def kernel(
    sizes,
    pairs_ref,
    x_hbm,
    proto_hbm,
    table_hbm,
    feed_hbm,
    keep_hbm,
    out_ref,
    x_ref,
    proto_ref,
    feed_ref,
    keep_ref,
    table_ref,
    place_ref,
    filt_ref,
    turn_out,
    turn_in,
    spill_one_out,
    spill_one_in,
    spill_two_out,
    spill_two_in,
    cat_ref,
    tile_out,
    tile_in,
    left_ref,
    right_ref,
    load_sem,
    turn_send,
    turn_recv,
    spill_send,
    spill_recv,
    tile_send,
    tile_recv,
):
    groups, n_tm, n_tile = sizes
    nodes = n_tm * n_tile
    me, tm, tile = lax.axis_index("freq"), lax.axis_index("tm"), lax.axis_index("tile")
    node = tm * n_tile + tile
    inputs, frames, points = x_hbm.shape

    def node_id(k):
        return (me, lax.div(k, n_tile), lax.rem(k, n_tile))

    loads = [
        pltpu.make_async_copy(src, dst, load_sem.at[i])
        for i, (src, dst) in enumerate(
            [
                (feed_hbm, feed_ref),
                (keep_hbm, keep_ref),
                (proto_hbm, proto_ref),
                (x_hbm, x_ref),
                (table_hbm, table_ref),
            ]
        )
    ]
    for load in loads:
        load.start()

    barrier = pltpu.get_barrier_semaphore()

    def greet_group(k, carry):
        pl.semaphore_signal(
            barrier, 1, device_id=(lax.rem(me + k, groups), tm, tile), device_id_type=MESH
        )
        return carry

    def greet_node(k, carry):
        pl.semaphore_signal(
            barrier, 1, device_id=node_id(lax.rem(node + k, nodes)), device_id_type=MESH
        )
        return carry

    before = lax.rem(node + nodes - 1, nodes)
    after = lax.rem(node + 1, nodes)

    def greet_before(k, carry):
        pl.semaphore_signal(
            barrier,
            1,
            device_id=(lax.rem(me + k, groups), lax.div(before, n_tile), lax.rem(before, n_tile)),
            device_id_type=MESH,
        )
        return carry

    lax.fori_loop(1, nodes, greet_node, 0)

    @pl.when(node > 0)
    def _():
        lax.fori_loop(0, groups, greet_before, 0)

    lax.fori_loop(1, groups, greet_group, 0)

    taps = proto_ref.shape[0]

    def column_of(row, first, size):
        lanes = lax.broadcasted_iota(jnp.int32, (size, LANES), 1)
        wanted = lax.broadcasted_iota(jnp.int32, (size, LANES), 0) + first
        picked = jnp.where(lanes == wanted, row.astype(jnp.float32), 0.0)
        return jnp.sum(picked, axis=1, keepdims=True)

    for load in loads[:4]:
        load.wait()
    per_row = LANES // inputs
    keep_row = keep_ref[pl.ds(lax.div(me, per_row), 1), :]
    keep = column_of(keep_row, lax.rem(me, per_row) * inputs, inputs)
    tiles_all = pairs_ref.shape[1]

    def build(k, carry):
        number = pairs_ref[lax.div(k, tiles_all), lax.rem(k, tiles_all)]
        row = feed_ref[pl.ds(lax.div(number, 2), 1), :]
        feeds = column_of(row, lax.rem(number, 2) * B, B).astype(jnp.int32)
        for q in range(2):
            place = lax.broadcasted_iota(jnp.int32, (1, groups * HALF), 1)
            source = lax.div(place, HALF) * inputs + lax.rem(place, HALF) + q * HALF
            place_ref[
                pl.ds(pl.multiple_of(k * B, B), B), q * groups * HALF : (q + 1) * groups * HALF
            ] = jnp.where(feeds == source, 1.0, 0.0).astype(jnp.bfloat16)
        return carry

    order = (3, 2, 6, 1, 0, 5, 4)

    def filter_columns(q, carry):
        cols = pl.ds(pl.multiple_of(q * 256, 256), 256)
        frame = [x_ref[:, k, cols].astype(jnp.float32) for k in range(frames)]
        for row, j in enumerate(order):
            total = None
            for lag in range(taps):
                if 0 <= j - lag < frames:
                    term = proto_ref[lag : lag + 1, cols] * frame[j - lag]
                    total = term if total is None else total + term
            filt_ref[row * inputs : (row + 1) * inputs, cols] = (total * keep).astype(
                jnp.bfloat16
            )
        return carry

    width = points // groups

    def channelize(q, carry):
        cols = pl.ds(pl.multiple_of(q * 256, 256), 256)
        y = jnp.dot(filt_ref[...], table_ref[:, cols], preferred_element_type=jnp.float32)

        def piece(first, size, b):
            return y[first : first + size, b * width : (b + 1) * width]

        def pair(row, b):
            pieces = [
                piece((row + f) * inputs + i * HALF, HALF, b) for i in range(2) for f in range(2)
            ]
            return jnp.concatenate(pieces, axis=1).astype(jnp.bfloat16)

        for b in range(256 // width):
            g = q * (256 // width) + b
            turn_out[0, g] = pair(0, b)
            turn_out[1, g] = pair(3, b)
            spill_two_out[g] = pair(5, b)
            eight = inputs // 4
            pieces = [piece(2 * inputs + i * eight, eight, b) for i in (1, 0, 3, 2)]
            spill_one_out[g] = jnp.concatenate(pieces, axis=1).astype(jnp.bfloat16)
        return carry

    spills = ((spill_one_out, spill_one_in), (spill_two_out, spill_two_in))

    def spill_copy(chunk, k):
        out, into = spills[chunk]
        peer = lax.rem(me + k, groups)
        return pltpu.make_async_remote_copy(
            src_ref=out.at[peer],
            dst_ref=into.at[me],
            send_sem=spill_send.at[chunk],
            recv_sem=spill_recv.at[chunk],
            device_id=(peer, lax.div(after, n_tile), lax.rem(after, n_tile)),
            device_id_type=MESH,
        )

    def spill_all(chunk):
        out, into = spills[chunk]
        return pltpu.make_async_remote_copy(
            src_ref=out,
            dst_ref=into,
            send_sem=spill_send.at[chunk],
            recv_sem=spill_recv.at[chunk],
            device_id=(me, lax.div(after, n_tile), lax.rem(after, n_tile)),
            device_id_type=MESH,
        )

    def send_spill(chunk):
        @pl.when(node < nodes - 1)
        def _():
            def go(k, carry):
                spill_copy(chunk, k).start()
                return carry

            lax.fori_loop(0, groups, go, 0)

    def wait_spill(chunk):
        into = spills[chunk][1]

        @pl.when(node == 0)
        def _():
            into[...] = jnp.zeros(into.shape, into.dtype)

        @pl.when(node > 0)
        def _():
            spill_all(chunk).wait_recv()

    def turn_copy(chunk, k):
        peer = lax.rem(me + k, groups)
        return pltpu.make_async_remote_copy(
            src_ref=turn_out.at[chunk, peer],
            dst_ref=turn_in.at[chunk, me],
            send_sem=turn_send.at[chunk],
            recv_sem=turn_recv.at[chunk],
            device_id=(peer, tm, tile),
            device_id_type=MESH,
        )

    def turn_all(chunk):
        return pltpu.make_async_remote_copy(
            src_ref=turn_out.at[chunk, pl.ds(0, groups - 1)],
            dst_ref=turn_in.at[chunk, pl.ds(0, groups - 1)],
            send_sem=turn_send.at[chunk],
            recv_sem=turn_recv.at[chunk],
            device_id=(lax.rem(me + 1, groups), tm, tile),
            device_id_type=MESH,
        )

    def send_turn(chunk):
        def go(k, carry):
            turn_copy(chunk, k).start()
            return carry

        lax.fori_loop(1, groups, go, 0)
        turn_in[chunk, me] = turn_out[chunk, me]

    def tile_copy(chunk, k):
        peer = lax.rem(node + k, nodes)
        return pltpu.make_async_remote_copy(
            src_ref=tile_out.at[chunk, peer],
            dst_ref=tile_in.at[chunk, node],
            send_sem=tile_send.at[chunk],
            recv_sem=tile_recv.at[chunk],
            device_id=node_id(peer),
            device_id_type=MESH,
        )

    def tile_all(chunk):
        return pltpu.make_async_remote_copy(
            src_ref=tile_out.at[chunk, pl.ds(0, nodes - 1)],
            dst_ref=tile_in.at[chunk, pl.ds(0, nodes - 1)],
            send_sem=tile_send.at[chunk],
            recv_sem=tile_recv.at[chunk],
            device_id=node_id(lax.rem(node + 1, nodes)),
            device_id_type=MESH,
        )

    rows_all = groups * HALF
    rows_node = tile_out.shape[2]
    per_step = 4

    def arrange(chunk):
        wait_spill(chunk)
        turn_all(chunk).wait_recv()
        block = turn_in[chunk].astype(jnp.float32)
        if chunk == 0:
            one = spill_one_in[...].astype(jnp.float32)
            lane = lax.broadcasted_iota(jnp.int32, one.shape, 2)
            odd = lax.rem(lax.div(lane, width), 2) == 1
            moved = jnp.where(odd, pltpu.roll(one, width, 2), 0.0)
            extra = jnp.concatenate([jnp.where(odd, one, 0.0), moved], axis=1)
        else:
            extra = spill_two_in[...].astype(jnp.float32)
        block = (block + extra).reshape(rows_all, LANES)
        cat_ref[0:rows_all] = block.astype(jnp.bfloat16)
        cat_ref[rows_all : 2 * rows_all] = pltpu.roll(block, B, 1).astype(jnp.bfloat16)
        low = lax.broadcasted_iota(jnp.int32, (per_step * rows_node, LANES), 1) < B

        def step(k, carry):
            size = per_step * rows_node
            first = pl.multiple_of(k * size, size)
            second = pl.multiple_of(nodes * rows_node + k * size, size)
            left = jnp.dot(
                place_ref[pl.ds(first, size), :], cat_ref[...], preferred_element_type=jnp.float32
            )
            right = jnp.dot(
                place_ref[pl.ds(second, size), :], cat_ref[...], preferred_element_type=jnp.float32
            )
            right = jnp.concatenate([right[:, B:], right[:, :B]], axis=1)
            both = jnp.where(low, left, right).astype(jnp.bfloat16)
            tile_out[chunk, pl.ds(k * per_step, per_step)] = both.reshape(
                per_step, rows_node, LANES
            )
            return carry

        lax.fori_loop(0, nodes // per_step, step, 0)

        def go(k, carry):
            tile_copy(chunk, k).start()
            return carry

        lax.fori_loop(1, nodes, go, 0)
        tile_in[chunk, node] = tile_out[chunk, node]

    lax.fori_loop(0, points // 256, filter_columns, 0)
    loads[4].wait()
    lax.fori_loop(0, points // 256, channelize, 0)
    expected = groups - 1 + nodes - 1 + jnp.where(node < nodes - 1, groups, 0)
    pl.semaphore_wait(barrier, expected)
    for chunk in range(2):
        send_spill(chunk)
        send_turn(chunk)
    lax.fori_loop(0, 2 * tiles_all, build, 0)
    arrange(0)
    arrange(1)

    tile_all(0).wait_recv()
    tile_all(1).wait_recv()
    lane = lax.broadcasted_iota(jnp.int32, (B, LANES), 1)
    low = lane < B
    channels = out_ref.shape[1]
    first_part = lax.rem(lane, 2 * channels) < channels
    shape = (channels, 1, nodes * LANES)
    own_lane = lax.rem(lax.broadcasted_iota(jnp.int32, shape, 2), channels)
    own_lane = own_lane == lax.broadcasted_iota(jnp.int32, shape, 0)
    own_lane = jnp.where(own_lane, 1.0, 0.0).astype(jnp.bfloat16)
    for t in range(out_ref.shape[0]):
        for k in range(nodes):
            one = tile_in[0, k, t * B : (t + 1) * B, :].astype(jnp.float32)
            two = tile_in[1, k, t * B : (t + 1) * B, :].astype(jnp.float32)
            one_turned = pltpu.roll(one, B, 1)
            two_turned = pltpu.roll(two, B, 1)
            left = jnp.where(low, one, two_turned)
            right = jnp.where(low, one_turned, two)
            cross = jnp.where(
                first_part, -pltpu.roll(right, LANES - channels, 1), pltpu.roll(right, channels, 1)
            )
            cols = slice(k * LANES, (k + 1) * LANES)
            left_ref[:, cols] = left.astype(jnp.bfloat16)
            right_ref[0:B, cols] = right.astype(jnp.bfloat16)
            right_ref[B : 2 * B, cols] = cross.astype(jnp.bfloat16)
        masked = (left_ref[...][None] * own_lane).reshape(channels * B, nodes * LANES)
        product = lax.dot_general(
            masked, right_ref[...], (((1,), (1,)), ((), ())), preferred_element_type=jnp.float32
        )
        out_ref[t] = (product * (1.0 / (frames * nodes))).reshape(channels, B, LANES)

    @pl.when(node < nodes - 1)
    def _():
        for chunk in range(2):
            spill_all(chunk).wait_send()

    for chunk in range(2):
        turn_all(chunk).wait_send()
        tile_all(chunk).wait_send()


def solution(mesh):
    groups, n_tm, n_tile = mesh.shape["freq"], mesh.shape["tm"], mesh.shape["tile"]
    nodes = n_tm * n_tile

    def shards(samples, prototype, feed_map, keep_mask, tile_pairs):
        taps = prototype.shape[0]
        inputs, frames, points = samples.shape
        total = inputs * groups
        tiles = tile_pairs.shape[0] // nodes
        channels = points // 2 // groups
        vmem = pl.BlockSpec(memory_space=pltpu.VMEM)
        bf = jnp.bfloat16
        body = lambda *refs: kernel((groups, n_tm, n_tile), *refs)
        return pl.pallas_call(
            body,
            out_shape=jax.ShapeDtypeStruct((tiles, channels, B, 2 * B), jnp.float32),
            in_specs=[pl.BlockSpec(memory_space=pltpu.SMEM)]
            + [pl.BlockSpec(memory_space=pltpu.HBM)] * 5,
            out_specs=vmem,
            scratch_shapes=[
                pltpu.VMEM((inputs, frames, points), bf),
                pltpu.VMEM((taps, points), jnp.float32),
                pltpu.VMEM((total // LANES, LANES), jnp.int32),
                pltpu.VMEM((total // LANES, LANES), jnp.int32),
                pltpu.VMEM((points, points), bf),
                pltpu.VMEM((total, total), bf),
                pltpu.VMEM((7 * inputs, points), bf),
                pltpu.VMEM((2, groups, HALF, LANES), bf),
                pltpu.VMEM((2, groups, HALF, LANES), bf),
                pltpu.VMEM((groups, HALF // 2, LANES), bf),
                pltpu.VMEM((groups, HALF // 2, LANES), bf),
                pltpu.VMEM((groups, HALF, LANES), bf),
                pltpu.VMEM((groups, HALF, LANES), bf),
                pltpu.VMEM((2 * groups * HALF, LANES), bf),
                pltpu.VMEM((2, nodes, tiles * B, LANES), bf),
                pltpu.VMEM((2, nodes, tiles * B, LANES), bf),
                pltpu.VMEM((B, nodes * LANES), bf),
                pltpu.VMEM((2 * B, nodes * LANES), bf),
                pltpu.SemaphoreType.DMA((5,)),
                pltpu.SemaphoreType.DMA((2,)),
                pltpu.SemaphoreType.DMA((2,)),
                pltpu.SemaphoreType.DMA((2,)),
                pltpu.SemaphoreType.DMA((2,)),
                pltpu.SemaphoreType.DMA((2,)),
                pltpu.SemaphoreType.DMA((2,)),
            ],
            compiler_params=pltpu.CompilerParams(
                collective_id=0, has_side_effects=True, vmem_limit_bytes=63 * 2**20
            ),
            cost_estimate=pl.CostEstimate(flops=4 * 10**9, bytes_accessed=10**7, transcendentals=0),
        )(
            tile_pairs.T,
            samples,
            prototype,
            dft_table(points, groups),
            feed_map.reshape(-1, LANES),
            keep_mask.reshape(-1, LANES),
        )

    return jax.shard_map(
        shards,
        mesh=mesh,
        in_specs=(P("freq", ("tm", "tile"), None), P(), P(), P(), P()),
        out_specs=P(("tm", "tile"), "freq", None, None),
        check_vma=False,
    )
```

```python
import functools
import math

import jax
import jax.numpy as jnp
import numpy as np
from jax import lax
from jax.experimental import pallas as pl
from jax.experimental.pallas import tpu as pltpu
from jax.sharding import PartitionSpec as P

MESH = pl.DeviceIdType.MESH
B = 64
HALF = 16
LANES = 128
STRIDE = 37


def dft_table(points, groups):
    per_group = points // 2 // groups
    column = np.arange(points)
    group, rest = column // (2 * per_group), column % (2 * per_group)
    part, channel = rest // per_group, group * per_group + rest % per_group
    angle = (np.arange(points)[:, None] * channel[None, :] % points) * (2.0 * math.pi / points)
    value = np.where(part[None, :] == 0, np.cos(angle), -np.sin(angle)) / math.sqrt(points)
    value = value.astype(np.float32).reshape(points, -1, 2 * LANES).transpose(1, 0, 2)
    return jnp.asarray(value).astype(jnp.bfloat16)


def kernel(
    sizes,
    pairs_ref,
    x_hbm,
    proto_hbm,
    table_hbm,
    feed_hbm,
    keep_hbm,
    tile_in,
    x_ref,
    proto_ref,
    feed_ref,
    keep_ref,
    table_ref,
    place_ref,
    filt_ref,
    turn_out,
    turn_in,
    spill_one_out,
    spill_one_in,
    spill_two_out,
    spill_two_in,
    cat_ref,
    tile_out,
    load_sem,
    table_sem,
    turn_send,
    turn_recv,
    spill_send,
    spill_recv,
    tile_send,
    tile_recv,
):
    groups, n_tm, n_tile = sizes
    nodes = n_tm * n_tile
    me, tm, tile = lax.axis_index("freq"), lax.axis_index("tm"), lax.axis_index("tile")
    node = tm * n_tile + tile
    inputs, frames, points = x_hbm.shape

    def node_id(k):
        return (me, lax.div(k, n_tile), lax.rem(k, n_tile))

    loads = [
        pltpu.make_async_copy(src, dst, load_sem.at[i])
        for i, (src, dst) in enumerate(
            [
                (feed_hbm, feed_ref),
                (keep_hbm, keep_ref),
                (proto_hbm, proto_ref),
                (x_hbm, x_ref),
            ]
        )
    ]
    for load in loads:
        load.start()

    blocks = table_ref.shape[0]

    def table_load(q):
        return pltpu.make_async_copy(table_hbm.at[q], table_ref.at[q], table_sem.at[q])

    def load_table(q, carry):
        table_load(q).start()
        return carry

    lax.fori_loop(0, blocks, load_table, 0)

    barrier = pltpu.get_barrier_semaphore()

    def greet_group(k, carry):
        pl.semaphore_signal(
            barrier, 1, device_id=(lax.rem(me + k, groups), tm, tile), device_id_type=MESH
        )
        return carry

    def greet_node(k, carry):
        pl.semaphore_signal(
            barrier, 1, device_id=node_id(lax.rem(node + k, nodes)), device_id_type=MESH
        )
        return carry

    before = lax.rem(node + nodes - 1, nodes)
    after = lax.rem(node + 1, nodes)

    def greet_before(k, carry):
        pl.semaphore_signal(
            barrier,
            1,
            device_id=(lax.rem(me + k, groups), lax.div(before, n_tile), lax.rem(before, n_tile)),
            device_id_type=MESH,
        )
        return carry

    lax.fori_loop(1, nodes, greet_node, 0)

    @pl.when(node > 0)
    def _():
        lax.fori_loop(0, groups, greet_before, 0)

    lax.fori_loop(1, groups, greet_group, 0)

    taps = proto_ref.shape[0]

    def column_of(row, first, size):
        lanes = lax.broadcasted_iota(jnp.int32, (size, LANES), 1)
        wanted = lax.broadcasted_iota(jnp.int32, (size, LANES), 0) + first
        picked = jnp.where(lanes == wanted, row.astype(jnp.float32), 0.0)
        return jnp.sum(picked, axis=1, keepdims=True)

    for load in loads:
        load.wait()
    per_row = LANES // inputs
    keep_row = keep_ref[pl.ds(lax.div(me, per_row), 1), :]
    keep = column_of(keep_row, lax.rem(me, per_row) * inputs, inputs)
    tiles_all = pairs_ref.shape[1]

    def build(k, carry):
        number = pairs_ref[lax.div(k, tiles_all), lax.rem(k, tiles_all)]
        row = feed_ref[pl.ds(lax.div(number, 2), 1), :]
        feeds = column_of(row, lax.rem(number, 2) * B, B).astype(jnp.int32)
        for q in range(2):
            place = lax.broadcasted_iota(jnp.int32, (1, groups * HALF), 1)
            source = lax.div(place, HALF) * inputs + lax.rem(place, HALF) + q * HALF
            place_ref[
                pl.ds(pl.multiple_of(k * B, B), B), q * groups * HALF : (q + 1) * groups * HALF
            ] = jnp.where(feeds == source, 1.0, 0.0).astype(jnp.bfloat16)
        return carry

    order = (3, 2, 6, 1, 0, 5, 4)

    def filter_columns(q, carry):
        cols = pl.ds(pl.multiple_of(q * 256, 256), 256)
        frame = [x_ref[:, k, cols].astype(jnp.float32) for k in range(frames)]
        for row, j in enumerate(order):
            total = None
            for lag in range(taps):
                if 0 <= j - lag < frames:
                    term = proto_ref[lag : lag + 1, cols] * frame[j - lag]
                    total = term if total is None else total + term
            filt_ref[row * inputs : (row + 1) * inputs, cols] = (total * keep).astype(
                jnp.bfloat16
            )
        return carry

    width = points // groups

    def channelize(q, carry):
        table_load(q).wait()
        y = jnp.dot(filt_ref[...], table_ref[q], preferred_element_type=jnp.float32)

        def piece(first, size, b):
            return y[first : first + size, b * width : (b + 1) * width]

        def pair(row, b):
            pieces = [
                piece((row + f) * inputs + i * HALF, HALF, b) for i in range(2) for f in range(2)
            ]
            return jnp.concatenate(pieces, axis=1).astype(jnp.bfloat16)

        for b in range(256 // width):
            g = q * (256 // width) + b
            turn_out[0, g] = pair(0, b)
            turn_out[1, g] = pair(3, b)
            spill_two_out[g] = pair(5, b)
            eight = inputs // 4
            pieces = [piece(2 * inputs + i * eight, eight, b) for i in (1, 0, 3, 2)]
            spill_one_out[g] = jnp.concatenate(pieces, axis=1).astype(jnp.bfloat16)
        return carry

    spills = ((spill_one_out, spill_one_in), (spill_two_out, spill_two_in))

    def spill_copy(chunk, k):
        out, into = spills[chunk]
        peer = lax.rem(me + k * STRIDE, groups)
        return pltpu.make_async_remote_copy(
            src_ref=out.at[peer],
            dst_ref=into.at[me],
            send_sem=spill_send.at[chunk],
            recv_sem=spill_recv.at[chunk],
            device_id=(peer, lax.div(after, n_tile), lax.rem(after, n_tile)),
            device_id_type=MESH,
        )

    def spill_all(chunk):
        out, into = spills[chunk]
        return pltpu.make_async_remote_copy(
            src_ref=out,
            dst_ref=into,
            send_sem=spill_send.at[chunk],
            recv_sem=spill_recv.at[chunk],
            device_id=(me, lax.div(after, n_tile), lax.rem(after, n_tile)),
            device_id_type=MESH,
        )

    def send_spill(chunk):
        @pl.when(node < nodes - 1)
        def _():
            def go(k, carry):
                spill_copy(chunk, k).start()
                return carry

            lax.fori_loop(0, groups, go, 0)

    def wait_spill(chunk):
        into = spills[chunk][1]

        @pl.when(node == 0)
        def _():
            into[...] = jnp.zeros(into.shape, into.dtype)

        @pl.when(node > 0)
        def _():
            spill_all(chunk).wait_recv()

    def turn_copy(chunk, k):
        peer = lax.rem(me + k * STRIDE, groups)
        return pltpu.make_async_remote_copy(
            src_ref=turn_out.at[chunk, peer],
            dst_ref=turn_in.at[chunk, me],
            send_sem=turn_send.at[chunk],
            recv_sem=turn_recv.at[chunk],
            device_id=(peer, tm, tile),
            device_id_type=MESH,
        )

    def turn_all(chunk):
        return pltpu.make_async_remote_copy(
            src_ref=turn_out.at[chunk, pl.ds(0, groups - 1)],
            dst_ref=turn_in.at[chunk, pl.ds(0, groups - 1)],
            send_sem=turn_send.at[chunk],
            recv_sem=turn_recv.at[chunk],
            device_id=(lax.rem(me + 1, groups), tm, tile),
            device_id_type=MESH,
        )

    def send_turn(chunk):
        def go(k, carry):
            turn_copy(chunk, k).start()
            return carry

        lax.fori_loop(1, groups, go, 0)
        turn_in[chunk, me] = turn_out[chunk, me]

    def wait_sent():
        @pl.when(node < nodes - 1)
        def _():
            for chunk in range(2):
                spill_all(chunk).wait_send()

        for chunk in range(2):
            turn_all(chunk).wait_send()

    def tile_copy(chunk, k):
        peer = lax.rem(node + k, nodes)
        return pltpu.make_async_remote_copy(
            src_ref=tile_out.at[chunk, peer],
            dst_ref=tile_in.at[chunk, node],
            send_sem=tile_send.at[chunk],
            recv_sem=tile_recv.at[chunk],
            device_id=node_id(peer),
            device_id_type=MESH,
        )

    def tile_all(chunk):
        return pltpu.make_async_remote_copy(
            src_ref=tile_out.at[chunk, pl.ds(0, nodes - 1)],
            dst_ref=tile_in.at[chunk, pl.ds(0, nodes - 1)],
            send_sem=tile_send.at[chunk],
            recv_sem=tile_recv.at[chunk],
            device_id=node_id(lax.rem(node + 1, nodes)),
            device_id_type=MESH,
        )

    rows_all = groups * HALF
    rows_node = tile_out.shape[2]
    per_step = 4

    def arrange(chunk):
        wait_spill(chunk)
        turn_all(chunk).wait_recv()
        block = turn_in[chunk].astype(jnp.float32)
        if chunk == 0:
            one = spill_one_in[...].astype(jnp.float32)
            lane = lax.broadcasted_iota(jnp.int32, one.shape, 2)
            odd = lax.rem(lax.div(lane, width), 2) == 1
            moved = jnp.where(odd, pltpu.roll(one, width, 2), 0.0)
            extra = jnp.concatenate([jnp.where(odd, one, 0.0), moved], axis=1)
        else:
            extra = spill_two_in[...].astype(jnp.float32)
        block = (block + extra).reshape(rows_all, LANES)
        cat_ref[0:rows_all] = block.astype(jnp.bfloat16)
        cat_ref[rows_all : 2 * rows_all] = pltpu.roll(block, B, 1).astype(jnp.bfloat16)
        low = lax.broadcasted_iota(jnp.int32, (per_step * rows_node, LANES), 1) < B

        def step(k, carry):
            size = per_step * rows_node
            first = pl.multiple_of(k * size, size)
            second = pl.multiple_of(nodes * rows_node + k * size, size)
            left = jnp.dot(
                place_ref[pl.ds(first, size), :], cat_ref[...], preferred_element_type=jnp.float32
            )
            right = jnp.dot(
                place_ref[pl.ds(second, size), :], cat_ref[...], preferred_element_type=jnp.float32
            )
            right = jnp.concatenate([right[:, B:], right[:, :B]], axis=1)
            both = jnp.where(low, left, right).astype(jnp.bfloat16)
            tile_out[chunk, pl.ds(k * per_step, per_step)] = both.reshape(
                per_step, rows_node, LANES
            )
            return carry

        lax.fori_loop(0, nodes // per_step, step, 0)
        if chunk == 0:
            wait_sent()

        def far(k, carry):
            tile_copy(chunk, 2 * k + 1).start()
            return carry

        def near(k, carry):
            tile_copy(chunk, 2 * k).start()
            return carry

        lax.fori_loop(0, nodes // 2, far, 0)
        lax.fori_loop(1, nodes // 2, near, 0)
        tile_in[chunk, node] = tile_out[chunk, node]

    lax.fori_loop(0, points // 256, filter_columns, 0)
    lax.fori_loop(0, blocks, channelize, 0)
    expected = groups - 1 + nodes - 1 + jnp.where(node < nodes - 1, groups, 0)
    pl.semaphore_wait(barrier, expected)
    send_spill(0)
    send_spill(1)
    send_turn(0)
    send_turn(1)
    lax.fori_loop(0, 2 * tiles_all, build, 0)
    arrange(0)
    arrange(1)

    tile_all(0).wait_recv()
    tile_all(1).wait_recv()

    tile_all(0).wait_send()
    tile_all(1).wait_send()


def correlate(scale, tile_in, out_ref, left_ref, right_ref):
    lane = lax.broadcasted_iota(jnp.int32, (B, LANES), 1)
    low = lane < B
    channels = out_ref.shape[1]
    nodes = tile_in.shape[1]
    first_part = lax.rem(lane, 2 * channels) < channels
    shape = (channels, 1, nodes * LANES)
    own_lane = lax.rem(lax.broadcasted_iota(jnp.int32, shape, 2), channels)
    own_lane = own_lane == lax.broadcasted_iota(jnp.int32, shape, 0)
    own_lane = jnp.where(own_lane, 1.0, 0.0).astype(jnp.bfloat16)
    for k in range(nodes):
        one = tile_in[0, k, :, :].astype(jnp.float32)
        two = tile_in[1, k, :, :].astype(jnp.float32)
        one_turned = pltpu.roll(one, B, 1)
        two_turned = pltpu.roll(two, B, 1)
        left = jnp.where(low, one, two_turned)
        right = jnp.where(low, one_turned, two)
        cross = jnp.where(
            first_part, -pltpu.roll(right, LANES - channels, 1), pltpu.roll(right, channels, 1)
        )
        cols = slice(k * LANES, (k + 1) * LANES)
        left_ref[:, cols] = left.astype(jnp.bfloat16)
        right_ref[0:B, cols] = right.astype(jnp.bfloat16)
        right_ref[B : 2 * B, cols] = cross.astype(jnp.bfloat16)
    masked = (left_ref[...][None] * own_lane).reshape(channels * B, nodes * LANES)
    product = lax.dot_general(
        masked, right_ref[...], (((1,), (1,)), ((), ())), preferred_element_type=jnp.float32
    )
    out_ref[0] = (product * scale).reshape(channels, B, LANES)


def solution(mesh):
    groups, n_tm, n_tile = mesh.shape["freq"], mesh.shape["tm"], mesh.shape["tile"]
    nodes = n_tm * n_tile

    def shards(samples, prototype, feed_map, keep_mask, tile_pairs):
        taps = prototype.shape[0]
        inputs, frames, points = samples.shape
        total = inputs * groups
        tiles = tile_pairs.shape[0] // nodes
        channels = points // 2 // groups
        table = dft_table(points, groups)
        vmem = pl.BlockSpec(memory_space=pltpu.VMEM)
        bf = jnp.bfloat16
        body = lambda *refs: kernel((groups, n_tm, n_tile), *refs)
        field = pl.pallas_call(
            body,
            out_shape=jax.ShapeDtypeStruct((2, nodes, tiles * B, LANES), bf),
            in_specs=[pl.BlockSpec(memory_space=pltpu.SMEM)]
            + [pl.BlockSpec(memory_space=pltpu.HBM)] * 5,
            out_specs=vmem,
            scratch_shapes=[
                pltpu.VMEM((inputs, frames, points), bf),
                pltpu.VMEM((taps, points), jnp.float32),
                pltpu.VMEM((total // LANES, LANES), jnp.int32),
                pltpu.VMEM((total // LANES, LANES), jnp.int32),
                pltpu.VMEM(table.shape, bf),
                pltpu.VMEM((total, total), bf),
                pltpu.VMEM((7 * inputs, points), bf),
                pltpu.VMEM((2, groups, HALF, LANES), bf),
                pltpu.VMEM((2, groups, HALF, LANES), bf),
                pltpu.VMEM((groups, HALF // 2, LANES), bf),
                pltpu.VMEM((groups, HALF // 2, LANES), bf),
                pltpu.VMEM((groups, HALF, LANES), bf),
                pltpu.VMEM((groups, HALF, LANES), bf),
                pltpu.VMEM((2 * groups * HALF, LANES), bf),
                pltpu.VMEM((2, nodes, tiles * B, LANES), bf),
                pltpu.SemaphoreType.DMA((4,)),
                pltpu.SemaphoreType.DMA((table.shape[0],)),
                pltpu.SemaphoreType.DMA((2,)),
                pltpu.SemaphoreType.DMA((2,)),
                pltpu.SemaphoreType.DMA((2,)),
                pltpu.SemaphoreType.DMA((2,)),
                pltpu.SemaphoreType.DMA((2,)),
                pltpu.SemaphoreType.DMA((2,)),
            ],
            compiler_params=pltpu.CompilerParams(
                collective_id=0, has_side_effects=True, vmem_limit_bytes=63 * 2**20
            ),
            cost_estimate=pl.CostEstimate(flops=4 * 10**9, bytes_accessed=10**7, transcendentals=0),
        )(
            tile_pairs.T,
            samples,
            prototype,
            table,
            feed_map.reshape(-1, LANES),
            keep_mask.reshape(-1, LANES),
        )

        return pl.pallas_call(
            functools.partial(correlate, 1.0 / (frames * nodes)),
            grid=(tiles,),
            out_shape=jax.ShapeDtypeStruct((tiles, channels, B, 2 * B), jnp.float32),
            in_specs=[pl.BlockSpec((2, nodes, B, LANES), lambda t: (0, 0, t, 0))],
            out_specs=pl.BlockSpec((1, channels, B, 2 * B), lambda t: (t, 0, 0, 0)),
            scratch_shapes=[
                pltpu.VMEM((B, nodes * LANES), bf),
                pltpu.VMEM((2 * B, nodes * LANES), bf),
            ],
            compiler_params=pltpu.CompilerParams(vmem_limit_bytes=32 * 2**20),
        )(field)

    return jax.shard_map(
        shards,
        mesh=mesh,
        in_specs=(P("freq", ("tm", "tile"), None), P(), P(), P(), P()),
        out_specs=P(("tm", "tile"), "freq", None, None),
        check_vma=False,
    )
```

```python
import functools
import math

import jax
import jax.numpy as jnp
import numpy as np
from jax import lax
from jax.experimental import pallas as pl
from jax.experimental.pallas import tpu as pltpu
from jax.sharding import PartitionSpec as P

MESH = pl.DeviceIdType.MESH
B = 64
HALF = 16
LANES = 128
STRIDE = 37


def dft_table(points, groups):
    per_group = points // 2 // groups
    column = np.arange(points)
    group, rest = column // (2 * per_group), column % (2 * per_group)
    part, channel = rest // per_group, group * per_group + rest % per_group
    angle = (np.arange(points)[:, None] * channel[None, :] % points) * (2.0 * math.pi / points)
    value = np.where(part[None, :] == 0, np.cos(angle), -np.sin(angle)) / math.sqrt(points)
    value = value.astype(np.float32).reshape(points, -1, 2 * LANES).transpose(1, 0, 2)
    return jnp.asarray(value).astype(jnp.bfloat16)


def kernel(
    sizes,
    pairs_ref,
    x_hbm,
    proto_hbm,
    table_hbm,
    feed_hbm,
    keep_hbm,
    tile_in,
    x_ref,
    proto_ref,
    feed_ref,
    keep_ref,
    table_ref,
    place_ref,
    filt_ref,
    turn_out,
    turn_in,
    spill_one_out,
    spill_one_in,
    spill_two_out,
    spill_two_in,
    cat_ref,
    tile_out,
    load_sem,
    table_sem,
    turn_send,
    turn_recv,
    spill_send,
    spill_recv,
    tile_send,
    tile_recv,
):
    groups, n_tm, n_tile = sizes
    nodes = n_tm * n_tile
    me, tm, tile = lax.axis_index("freq"), lax.axis_index("tm"), lax.axis_index("tile")
    node = tm * n_tile + tile
    inputs, frames, points = x_hbm.shape

    def node_id(k):
        return (me, lax.div(k, n_tile), lax.rem(k, n_tile))

    loads = [
        pltpu.make_async_copy(src, dst, load_sem.at[i])
        for i, (src, dst) in enumerate(
            [
                (feed_hbm, feed_ref),
                (keep_hbm, keep_ref),
                (proto_hbm, proto_ref),
                (x_hbm, x_ref),
            ]
        )
    ]
    for load in loads:
        load.start()

    blocks = table_ref.shape[0]

    def table_load(q):
        return pltpu.make_async_copy(table_hbm.at[q], table_ref.at[q], table_sem.at[q])

    def load_table(q, carry):
        table_load(q).start()
        return carry

    lax.fori_loop(0, blocks, load_table, 0)

    barrier = pltpu.get_barrier_semaphore()

    def greet_group(k, carry):
        pl.semaphore_signal(
            barrier, 1, device_id=(lax.rem(me + k, groups), tm, tile), device_id_type=MESH
        )
        return carry

    def greet_node(k, carry):
        pl.semaphore_signal(
            barrier, 1, device_id=node_id(lax.rem(node + k, nodes)), device_id_type=MESH
        )
        return carry

    before = lax.rem(node + nodes - 1, nodes)
    after = lax.rem(node + 1, nodes)

    def greet_before(k, carry):
        pl.semaphore_signal(
            barrier,
            1,
            device_id=(lax.rem(me + k, groups), lax.div(before, n_tile), lax.rem(before, n_tile)),
            device_id_type=MESH,
        )
        return carry

    lax.fori_loop(1, nodes, greet_node, 0)

    @pl.when(node > 0)
    def _():
        lax.fori_loop(0, groups, greet_before, 0)

    lax.fori_loop(1, groups, greet_group, 0)

    taps = proto_ref.shape[0]

    def column_of(row, first, size):
        lanes = lax.broadcasted_iota(jnp.int32, (size, LANES), 1)
        wanted = lax.broadcasted_iota(jnp.int32, (size, LANES), 0) + first
        picked = jnp.where(lanes == wanted, row.astype(jnp.float32), 0.0)
        return jnp.sum(picked, axis=1, keepdims=True)

    for load in loads:
        load.wait()
    per_row = LANES // inputs
    keep_row = keep_ref[pl.ds(lax.div(me, per_row), 1), :]
    keep = column_of(keep_row, lax.rem(me, per_row) * inputs, inputs)
    tiles_all = pairs_ref.shape[1]

    def build(k, carry):
        number = pairs_ref[lax.div(k, tiles_all), lax.rem(k, tiles_all)]
        row = feed_ref[pl.ds(lax.div(number, 2), 1), :]
        feeds = column_of(row, lax.rem(number, 2) * B, B).astype(jnp.int32)
        for q in range(2):
            place = lax.broadcasted_iota(jnp.int32, (1, groups * HALF), 1)
            source = lax.div(place, HALF) * inputs + lax.rem(place, HALF) + q * HALF
            place_ref[
                pl.ds(pl.multiple_of(k * B, B), B), q * groups * HALF : (q + 1) * groups * HALF
            ] = jnp.where(feeds == source, 1.0, 0.0).astype(jnp.bfloat16)
        return carry

    order = (6, 5, 4, 3, 2, 1, 0)
    spilled = taps - 1

    def filter_columns(rows, q, carry):
        cols = pl.ds(pl.multiple_of(q * 256, 256), 256)
        frame = [x_ref[:, k, cols].astype(jnp.float32) for k in range(frames)]
        for row in rows:
            j = order[row]
            total = None
            for lag in range(taps):
                if 0 <= j - lag < frames:
                    term = proto_ref[lag : lag + 1, cols] * frame[j - lag]
                    total = term if total is None else total + term
            filt_ref[row * inputs : (row + 1) * inputs, cols] = (total * keep).astype(
                jnp.bfloat16
            )
        return carry


    width = points // groups
    per_block = groups // blocks

    def multiply(q, first, count):
        rows = slice(first * inputs, (first + count) * inputs)
        return jnp.dot(filt_ref[rows, :], table_ref[q], preferred_element_type=jnp.float32)

    def pair(y, row, b):
        pieces = [
            y[(row + f) * inputs + i * HALF :, b * width : (b + 1) * width][:HALF]
            for i in range(2)
            for f in range(2)
        ]
        return jnp.concatenate(pieces, axis=1).astype(jnp.bfloat16)

    def channelize_spilled(q, carry):
        table_load(q).wait()
        y = multiply(q, 0, spilled)
        eight = inputs // 4
        for b in range(per_block):
            spill_two_out[q * per_block + b] = pair(y, 1, b)
            pieces = [
                y[i * eight : (i + 1) * eight, b * width : (b + 1) * width] for i in (1, 0, 3, 2)
            ]
            spill_one_out[q * per_block + b] = jnp.concatenate(pieces, axis=1).astype(
                jnp.bfloat16
            )
        return carry

    def channelize_own(q, carry):
        y = multiply(q, spilled, frames)
        for b in range(per_block):
            turn_out[0, q * per_block + b] = pair(y, 0, b)
            turn_out[1, q * per_block + b] = pair(y, 2, b)
        return carry

    spills = ((spill_one_out, spill_one_in), (spill_two_out, spill_two_in))

    def spill_copy(chunk, k):
        out, into = spills[chunk]
        peer = lax.rem(me + k * STRIDE, groups)
        return pltpu.make_async_remote_copy(
            src_ref=out.at[peer],
            dst_ref=into.at[me],
            send_sem=spill_send.at[chunk],
            recv_sem=spill_recv.at[chunk],
            device_id=(peer, lax.div(after, n_tile), lax.rem(after, n_tile)),
            device_id_type=MESH,
        )

    def spill_all(chunk):
        out, into = spills[chunk]
        return pltpu.make_async_remote_copy(
            src_ref=out,
            dst_ref=into,
            send_sem=spill_send.at[chunk],
            recv_sem=spill_recv.at[chunk],
            device_id=(me, lax.div(after, n_tile), lax.rem(after, n_tile)),
            device_id_type=MESH,
        )

    def send_spill(chunk):
        @pl.when(node < nodes - 1)
        def _():
            def go(k, carry):
                spill_copy(chunk, k).start()
                return carry

            lax.fori_loop(0, groups, go, 0)

    def wait_spill(chunk):
        into = spills[chunk][1]

        @pl.when(node == 0)
        def _():
            into[...] = jnp.zeros(into.shape, into.dtype)

        @pl.when(node > 0)
        def _():
            spill_all(chunk).wait_recv()

    def turn_copy(chunk, k):
        peer = lax.rem(me + k * STRIDE, groups)
        return pltpu.make_async_remote_copy(
            src_ref=turn_out.at[chunk, peer],
            dst_ref=turn_in.at[chunk, me],
            send_sem=turn_send.at[chunk],
            recv_sem=turn_recv.at[chunk],
            device_id=(peer, tm, tile),
            device_id_type=MESH,
        )

    def turn_all(chunk):
        return pltpu.make_async_remote_copy(
            src_ref=turn_out.at[chunk, pl.ds(0, groups - 1)],
            dst_ref=turn_in.at[chunk, pl.ds(0, groups - 1)],
            send_sem=turn_send.at[chunk],
            recv_sem=turn_recv.at[chunk],
            device_id=(lax.rem(me + 1, groups), tm, tile),
            device_id_type=MESH,
        )

    def send_turn(chunk):
        def go(k, carry):
            turn_copy(chunk, k).start()
            return carry

        lax.fori_loop(1, groups, go, 0)
        turn_in[chunk, me] = turn_out[chunk, me]

    def wait_sent():
        @pl.when(node < nodes - 1)
        def _():
            for chunk in range(2):
                spill_all(chunk).wait_send()

        for chunk in range(2):
            turn_all(chunk).wait_send()

    def tile_copy(chunk, k):
        peer = lax.rem(node + k, nodes)
        return pltpu.make_async_remote_copy(
            src_ref=tile_out.at[chunk, peer],
            dst_ref=tile_in.at[chunk, node],
            send_sem=tile_send.at[chunk],
            recv_sem=tile_recv.at[chunk],
            device_id=node_id(peer),
            device_id_type=MESH,
        )

    def tile_all(chunk):
        return pltpu.make_async_remote_copy(
            src_ref=tile_out.at[chunk, pl.ds(0, nodes - 1)],
            dst_ref=tile_in.at[chunk, pl.ds(0, nodes - 1)],
            send_sem=tile_send.at[chunk],
            recv_sem=tile_recv.at[chunk],
            device_id=node_id(lax.rem(node + 1, nodes)),
            device_id_type=MESH,
        )

    rows_all = groups * HALF
    rows_node = tile_out.shape[2]
    per_step = 4

    def arrange(chunk):
        wait_spill(chunk)
        turn_all(chunk).wait_recv()
        block = turn_in[chunk].astype(jnp.float32)
        if chunk == 0:
            one = spill_one_in[...].astype(jnp.float32)
            lane = lax.broadcasted_iota(jnp.int32, one.shape, 2)
            odd = lax.rem(lax.div(lane, width), 2) == 1
            moved = jnp.where(odd, pltpu.roll(one, width, 2), 0.0)
            extra = jnp.concatenate([jnp.where(odd, one, 0.0), moved], axis=1)
        else:
            extra = spill_two_in[...].astype(jnp.float32)
        block = (block + extra).reshape(rows_all, LANES)
        cat_ref[0:rows_all] = block.astype(jnp.bfloat16)
        cat_ref[rows_all : 2 * rows_all] = pltpu.roll(block, B, 1).astype(jnp.bfloat16)
        low = lax.broadcasted_iota(jnp.int32, (per_step * rows_node, LANES), 1) < B

        def step(k, carry):
            size = per_step * rows_node
            first = pl.multiple_of(k * size, size)
            second = pl.multiple_of(nodes * rows_node + k * size, size)
            left = jnp.dot(
                place_ref[pl.ds(first, size), :], cat_ref[...], preferred_element_type=jnp.float32
            )
            right = jnp.dot(
                place_ref[pl.ds(second, size), :], cat_ref[...], preferred_element_type=jnp.float32
            )
            right = jnp.concatenate([right[:, B:], right[:, :B]], axis=1)
            both = jnp.where(low, left, right).astype(jnp.bfloat16)
            tile_out[chunk, pl.ds(k * per_step, per_step)] = both.reshape(
                per_step, rows_node, LANES
            )
            return carry

        lax.fori_loop(0, nodes // per_step, step, 0)
        if chunk == 0:
            wait_sent()

        def far(k, carry):
            tile_copy(chunk, 2 * k + 1).start()
            return carry

        def near(k, carry):
            tile_copy(chunk, 2 * k).start()
            return carry

        lax.fori_loop(0, nodes // 2, far, 0)
        lax.fori_loop(1, nodes // 2, near, 0)
        tile_in[chunk, node] = tile_out[chunk, node]

    first_rows, own_rows = range(spilled), range(spilled, spilled + frames)
    lax.fori_loop(0, points // 256, functools.partial(filter_columns, first_rows), 0)
    lax.fori_loop(0, blocks, channelize_spilled, 0)
    expected = groups - 1 + nodes - 1 + jnp.where(node < nodes - 1, groups, 0)
    pl.semaphore_wait(barrier, expected)
    send_spill(0)
    send_spill(1)
    lax.fori_loop(0, points // 256, functools.partial(filter_columns, own_rows), 0)
    lax.fori_loop(0, blocks, channelize_own, 0)
    send_turn(0)
    send_turn(1)
    lax.fori_loop(0, 2 * tiles_all, build, 0)
    arrange(0)
    arrange(1)

    tile_all(0).wait_recv()
    tile_all(1).wait_recv()

    tile_all(0).wait_send()
    tile_all(1).wait_send()


def correlate(scale, tile_in, out_ref, left_ref, right_ref):
    lane = lax.broadcasted_iota(jnp.int32, (B, LANES), 1)
    low = lane < B
    channels = out_ref.shape[1]
    nodes = tile_in.shape[1]
    first_part = lax.rem(lane, 2 * channels) < channels
    shape = (channels, 1, nodes * LANES)
    own_lane = lax.rem(lax.broadcasted_iota(jnp.int32, shape, 2), channels)
    own_lane = own_lane == lax.broadcasted_iota(jnp.int32, shape, 0)
    own_lane = jnp.where(own_lane, 1.0, 0.0).astype(jnp.bfloat16)
    for k in range(nodes):
        one = tile_in[0, k, :, :].astype(jnp.float32)
        two = tile_in[1, k, :, :].astype(jnp.float32)
        one_turned = pltpu.roll(one, B, 1)
        two_turned = pltpu.roll(two, B, 1)
        left = jnp.where(low, one, two_turned)
        right = jnp.where(low, one_turned, two)
        cross = jnp.where(
            first_part, -pltpu.roll(right, LANES - channels, 1), pltpu.roll(right, channels, 1)
        )
        cols = slice(k * LANES, (k + 1) * LANES)
        left_ref[:, cols] = left.astype(jnp.bfloat16)
        right_ref[0:B, cols] = right.astype(jnp.bfloat16)
        right_ref[B : 2 * B, cols] = cross.astype(jnp.bfloat16)
    masked = (left_ref[...][None] * own_lane).reshape(channels * B, nodes * LANES)
    product = lax.dot_general(
        masked, right_ref[...], (((1,), (1,)), ((), ())), preferred_element_type=jnp.float32
    )
    out_ref[0] = (product * scale).reshape(channels, B, LANES)


def solution(mesh):
    groups, n_tm, n_tile = mesh.shape["freq"], mesh.shape["tm"], mesh.shape["tile"]
    nodes = n_tm * n_tile

    def shards(samples, prototype, feed_map, keep_mask, tile_pairs):
        taps = prototype.shape[0]
        inputs, frames, points = samples.shape
        total = inputs * groups
        tiles = tile_pairs.shape[0] // nodes
        channels = points // 2 // groups
        table = dft_table(points, groups)
        vmem = pl.BlockSpec(memory_space=pltpu.VMEM)
        bf = jnp.bfloat16
        body = lambda *refs: kernel((groups, n_tm, n_tile), *refs)
        field = pl.pallas_call(
            body,
            out_shape=jax.ShapeDtypeStruct((2, nodes, tiles * B, LANES), bf),
            in_specs=[pl.BlockSpec(memory_space=pltpu.SMEM)]
            + [pl.BlockSpec(memory_space=pltpu.HBM)] * 5,
            out_specs=vmem,
            scratch_shapes=[
                pltpu.VMEM((inputs, frames, points), bf),
                pltpu.VMEM((taps, points), jnp.float32),
                pltpu.VMEM((total // LANES, LANES), jnp.int32),
                pltpu.VMEM((total // LANES, LANES), jnp.int32),
                pltpu.VMEM(table.shape, bf),
                pltpu.VMEM((total, total), bf),
                pltpu.VMEM((7 * inputs, points), bf),
                pltpu.VMEM((2, groups, HALF, LANES), bf),
                pltpu.VMEM((2, groups, HALF, LANES), bf),
                pltpu.VMEM((groups, HALF // 2, LANES), bf),
                pltpu.VMEM((groups, HALF // 2, LANES), bf),
                pltpu.VMEM((groups, HALF, LANES), bf),
                pltpu.VMEM((groups, HALF, LANES), bf),
                pltpu.VMEM((2 * groups * HALF, LANES), bf),
                pltpu.VMEM((2, nodes, tiles * B, LANES), bf),
                pltpu.SemaphoreType.DMA((4,)),
                pltpu.SemaphoreType.DMA((table.shape[0],)),
                pltpu.SemaphoreType.DMA((2,)),
                pltpu.SemaphoreType.DMA((2,)),
                pltpu.SemaphoreType.DMA((2,)),
                pltpu.SemaphoreType.DMA((2,)),
                pltpu.SemaphoreType.DMA((2,)),
                pltpu.SemaphoreType.DMA((2,)),
            ],
            compiler_params=pltpu.CompilerParams(
                collective_id=0, has_side_effects=True, vmem_limit_bytes=63 * 2**20
            ),
            cost_estimate=pl.CostEstimate(flops=4 * 10**9, bytes_accessed=10**7, transcendentals=0),
        )(
            tile_pairs.T,
            samples,
            prototype,
            table,
            feed_map.reshape(-1, LANES),
            keep_mask.reshape(-1, LANES),
        )

        return pl.pallas_call(
            functools.partial(correlate, 1.0 / (frames * nodes)),
            grid=(tiles,),
            out_shape=jax.ShapeDtypeStruct((tiles, channels, B, 2 * B), jnp.float32),
            in_specs=[pl.BlockSpec((2, nodes, B, LANES), lambda t: (0, 0, t, 0))],
            out_specs=pl.BlockSpec((1, channels, B, 2 * B), lambda t: (t, 0, 0, 0)),
            scratch_shapes=[
                pltpu.VMEM((B, nodes * LANES), bf),
                pltpu.VMEM((2 * B, nodes * LANES), bf),
            ],
            compiler_params=pltpu.CompilerParams(vmem_limit_bytes=32 * 2**20),
        )(field)

    return jax.shard_map(
        shards,
        mesh=mesh,
        in_specs=(P("freq", ("tm", "tile"), None), P(), P(), P(), P()),
        out_specs=P(("tm", "tile"), "freq", None, None),
        check_vma=False,
    )
```
